32 devices in a mesh: lat: 8 (over y, x, core), lev: 4 (over z).
Axes of the slice: x: 2, y: 2, z: 4, core: 2. Of those that a mesh axis runs over, the one named last changes fastest.
Arguments:
- fields: float32 [6, 60, 32, 1024], P(None, 'lev', 'lat'), may hold values from -6 to 6
- zonal_courant: float32 [60, 32], replicated, may hold values from -0.16 to 0.16
- merid_courant: float32 [60, 31], replicated, may hold values from -0.16 to 0.16
- vert_courant: float32 [59, 32], replicated, may hold values from -0.16 to 0.16
- column_class: int32 [32, 1024], replicated, may hold values from 1 to 4, as said below
- in_gain: float32 [360], replicated, may hold values from 0.1 to 1.9
- w_in: bfloat16 [360, 1024], replicated, may hold values from -0.3125 to 0.3125
- w_up: bfloat16 [1, 1024, 1024], replicated, may hold values from -0.1875 to 0.1875
- w_down: bfloat16 [1, 1024, 1024], replicated, may hold values from -0.1875 to 0.1875
- out_gain: float32 [1024], replicated, may hold values from 0.1 to 1.9
- w_out: bfloat16 [1024, 360], replicated, may hold values from -0.1875 to 0.1875
Outputs:
- fields_out: float32 [6, 60, 32, 1024], P(None, 'lev', 'lat')
The draws below stay inside these ranges and needn't reach their ends.
Inputs may be any that keep to these rules, and one draw needn't show every extreme that they name: column_class is the number of physics substeps of a column; some column has 4 in every draw.
All inputs are finite; a program needn't handle non-finite values.
Results may differ from the reference program's by a relative error of at most 0.0042.
Values sent between devices are 32-bit elements; how exact they have to be, the bound alone decides.
A program may use at most 128 MiB of HBM per device.

```python
import jax
import jax.numpy as jnp
from jax import lax

FIELDS = 6
LEVELS = 60
UNITS = 1024
LAYERS = 1
KMAX = 4
STEPS = 2
LON = 1024
LATS = 32
NIN = 360


def draw_column_class(key, part):
    band_key, heavy_key, light_key = jax.random.split(key, 3)
    start = jax.random.randint(band_key, (), 0, LATS)
    rows = jnp.arange(LATS)
    inside = jnp.mod(rows - start, LATS) < LATS // 4
    heavy = jax.random.randint(heavy_key, (LATS, LON), 1, KMAX + 1)
    light = 1 + (jax.random.randint(light_key, (LATS, LON), 0, 50) == 0).astype(jnp.int32)
    classes = jnp.where(inside[:, None], heavy, light)
    classes = classes.at[start, 0].set(KMAX)
    return classes.astype(jnp.int32)


def block_levels(stream_key, extent, cuts, least, top_value):
    level, own = 1.0, jax.random.fold_in(stream_key, 6)
    for dim, shards_of in cuts:
        draws = jnp.exp(jax.random.uniform(jax.random.fold_in(own, dim), (shards_of,), jnp.float32, least / len(cuts), top_value / len(cuts)))
        level = level * jnp.repeat(draws, extent[dim] // shards_of).reshape([-1 if axis == dim else 1 for axis in range(len(extent))])
    return level


def normal_values(own_key, dims, width, bound, cuts=(), held_as=jnp.bfloat16):
    loudness = block_levels(own_key, dims, cuts, -0.22, 0.18) if cuts else 1.0
    entries = jax.random.normal(own_key, dims, jnp.float32) * width * loudness
    return jnp.minimum(jnp.maximum(entries, -bound), bound).astype(held_as)


def setup_inputs(seed: int = 0) -> dict:
    key_of = jax.random.split(jax.random.key(seed), 12)
    return {
        "fields": normal_values(key_of[0], (FIELDS, LEVELS, LATS, LON), 1.0, 6.0, ((1, 4), (2, 8)), jnp.float32),
        "zonal_courant": jnp.clip(jax.random.uniform(key_of[1], (LEVELS, LATS), jnp.float32, -0.16, 0.16), -0.16, 0.16),
        "merid_courant": jnp.clip(jax.random.uniform(key_of[2], (LEVELS, LATS - 1), jnp.float32, -0.16, 0.16), -0.16, 0.16),
        "vert_courant": jnp.clip(jax.random.uniform(key_of[3], (LEVELS - 1, LATS), jnp.float32, -0.16, 0.16), -0.16, 0.16),
        "column_class": draw_column_class(jax.random.fold_in(key_of[11], 71), 0),
        "in_gain": jnp.clip(1.0 + 0.18 * jax.random.normal(key_of[5], (NIN,), jnp.float32), 0.1, 1.9),
        "w_in": normal_values(key_of[6], (NIN, UNITS), NIN ** -0.5, 0.3125),
        "w_up": normal_values(key_of[7], (LAYERS, UNITS, UNITS), UNITS ** -0.5, 0.1875),
        "w_down": normal_values(key_of[8], (LAYERS, UNITS, UNITS), UNITS ** -0.5, 0.1875),
        "out_gain": jnp.clip(1.0 + 0.18 * jax.random.normal(key_of[9], (UNITS,), jnp.float32), 0.1, 1.9),
        "w_out": normal_values(key_of[10], (UNITS, NIN), UNITS ** -0.5, 0.1875),
    }


def upwind(courant, behind, ahead):
    return jnp.maximum(courant, 0.0) * behind + jnp.minimum(courant, 0.0) * ahead

def transport(state, zonal, merid, vertical):
    east = upwind(zonal[None, :, :, None], state, jnp.roll(state, -1, axis=3))
    zonal_change = east - jnp.roll(east, 1, axis=3)
    rows_padded = jnp.pad(state, ((0, 0), (0, 0), (1, 1), (0, 0)))
    north = upwind(merid[None, :, :, None], rows_padded[:, :, :-1], rows_padded[:, :, 1:])
    merid_change = north[:, :, 1:] - north[:, :, :-1]
    levels_padded = jnp.pad(state, ((0, 0), (1, 1), (0, 0), (0, 0)))
    downward = upwind(vertical[None, :, :, None], levels_padded[:, :-1], levels_padded[:, 1:])
    vertical_change = downward[:, 1:] - downward[:, :-1]
    return state - (zonal_change + merid_change + vertical_change)

def rms_scaled(values):
    return values * lax.rsqrt(lax.optimization_barrier(jnp.mean(values * values, axis=0, keepdims=True)) + 1e-06)

def contract(weight, values):
    return lax.dot_general(weight, values, (((0,), (0,)), ((), ())), preferred_element_type=jnp.float32)

def tendency(state, in_gain, w_in, w_up, w_down, out_gain, w_out):
    normed = (rms_scaled(state) * in_gain[:, None]).astype(jnp.bfloat16)
    hidden = contract(w_in, normed)
    for layer in range(w_up.shape[0]):
        inner = rms_scaled(hidden).astype(jnp.bfloat16)
        gated = jax.nn.silu(contract(w_up[layer], inner)).astype(jnp.bfloat16)
        hidden = hidden + contract(w_down[layer], gated)
    final = (rms_scaled(hidden) * out_gain[:, None]).astype(jnp.bfloat16)
    return contract(w_out, final)

def substeps(state, classes, weights):
    trips = jnp.max(classes)

    def advance(counter, current):
        change = tendency(current, *weights)
        return current + jnp.where(classes[None, :] > counter, change, 0.0)
    return lax.fori_loop(jnp.int32(0), trips, advance, state)

def reference(fields, zonal_courant, merid_courant, vert_courant, column_class, in_gain, w_in, w_up, w_down, out_gain, w_out):
    merid = jnp.pad(merid_courant, ((0, 0), (1, 1)))
    vertical = jnp.pad(vert_courant, ((1, 1), (0, 0)))
    state = fields
    for step in range(STEPS):
        state = transport(state, zonal_courant, merid, vertical)
    columns = state.reshape(FIELDS * LEVELS, LATS, LON).transpose(1, 0, 2)
    weights = (in_gain, w_in, w_up, w_down, out_gain, w_out)

    def run_row(item):
        return substeps(item[0], item[1], weights)
    finished = lax.map(run_row, (columns, column_class))
    return finished.transpose(1, 0, 2).reshape(FIELDS, LEVELS, LATS, LON)
```

```python
import functools

import jax
import jax.numpy as jnp
from jax import lax
from jax.experimental import pallas as pl
from jax.experimental.pallas import tpu as pltpu
from jax.sharding import PartitionSpec as P

STEPS = 2
SUBSTEPS = 4
MESH = pl.DeviceIdType.MESH


def with_halo(cells, sides, width):
    for axis, dim in sides:
        count = lax.axis_size(axis)
        ends = count - 1
        head = lax.slice_in_dim(cells, 0, width, axis=dim)
        tail = lax.slice_in_dim(cells, cells.shape[dim] - width, cells.shape[dim], axis=dim)
        cells = jnp.concatenate(
            [
                lax.ppermute(tail, axis, [(i, (i + 1) % count) for i in range(ends)]),
                cells,
                lax.ppermute(head, axis, [((i + 1) % count, i) for i in range(ends)]),
            ],
            axis=dim,
        )
    return cells


def upwind(courant, behind, ahead):
    return jnp.maximum(courant, 0.0) * behind + jnp.minimum(courant, 0.0) * ahead


def transport(state, zonal, merid, vertical):
    east = upwind(zonal[None, :, :, None], state, jnp.roll(state, -1, axis=3))
    zonal_change = east - jnp.roll(east, 1, axis=3)
    rows_padded = jnp.pad(state, ((0, 0), (0, 0), (1, 1), (0, 0)))
    north = upwind(merid[None, :, :, None], rows_padded[:, :, :-1], rows_padded[:, :, 1:])
    merid_change = north[:, :, 1:] - north[:, :, :-1]
    levels_padded = jnp.pad(state, ((0, 0), (1, 1), (0, 0), (0, 0)))
    downward = upwind(vertical[None, :, :, None], levels_padded[:, :-1], levels_padded[:, 1:])
    vertical_change = downward[:, 1:] - downward[:, :-1]
    return state - (zonal_change + merid_change + vertical_change)


def face_winds(
    zonal_courant, merid_courant, vert_courant, width, lev_start, row_start, levels_here, rows_here
):
    zonal = jnp.pad(zonal_courant, ((width, width), (width, width)))
    zonal = lax.dynamic_slice(
        zonal, (lev_start, row_start), (levels_here + 2 * width, rows_here + 2 * width)
    )
    merid = jnp.pad(merid_courant, ((width, width), (width + 1, width + 1)))
    merid = lax.dynamic_slice(
        merid, (lev_start, row_start), (levels_here + 2 * width, rows_here + 2 * width + 1)
    )
    vertical = jnp.pad(vert_courant, ((width + 1, width + 1), (width, width)))
    vertical = lax.dynamic_slice(
        vertical, (lev_start, row_start), (levels_here + 2 * width + 1, rows_here + 2 * width)
    )
    return (zonal, merid, vertical)


def inverse_rms(values, entries):
    return lax.rsqrt(jnp.sum(values * values, axis=0, keepdims=True) / entries + 1e-06)


def dot(a, b):
    return jnp.dot(a, b, preferred_element_type=jnp.float32)


def physics_kernel(
    n, entries,
    state, classes, in_gain, w_in, w_up, w_down, out_gain, w_out,
    out,
    held, fsend, frecv, bsend, brecv,
):
    me = lax.axis_index("lev")
    rows, depth, lons = state.shape
    quarter = lons // n

    barrier = pltpu.get_barrier_semaphore()
    for d in range(1, n):
        pl.semaphore_signal(barrier, inc=1, device_id={"lev": lax.rem(me + d, n)}, device_id_type=MESH)
    pl.semaphore_wait(barrier, n - 1)

    own = pl.ds(pl.multiple_of(me * quarter, quarter), quarter)

    def forward(r, d):
        peer = lax.rem(me + d, n)
        there = pl.ds(pl.multiple_of(peer * quarter, quarter), quarter)
        return pltpu.make_async_remote_copy(
            src_ref=state.at[r, :, there],
            dst_ref=held.at[r, me],
            send_sem=fsend.at[r, d - 1],
            recv_sem=frecv.at[r, d - 1],
            device_id={"lev": peer},
            device_id_type=MESH,
        )

    def backward(r, d):
        peer = lax.rem(me + d, n)
        return pltpu.make_async_remote_copy(
            src_ref=held.at[r, peer],
            dst_ref=out.at[r, :, own],
            send_sem=bsend.at[r, d - 1],
            recv_sem=brecv.at[r, d - 1],
            device_id={"lev": peer},
            device_id_type=MESH,
        )

    for r in range(rows):
        for d in range(1, n):
            forward(r, d).start()

    def one_row(r, carry):
        held[r, me] = state[r, :, own]
        for d in range(1, n):
            forward(r, d).wait_recv()

        def substep(s, carry):
            x = held[r].reshape(n * depth, quarter)
            a = (x * inverse_rms(x, entries) * in_gain[...]).astype(jnp.bfloat16)
            h = dot(w_in[...], a)
            units = h.shape[0]
            g = (h * inverse_rms(h, units)).astype(jnp.bfloat16)
            v = dot(w_up[...], g)
            u = (v / (1.0 + jnp.exp(-v))).astype(jnp.bfloat16)
            h = h + dot(w_down[...], u)
            z = (h * inverse_rms(h, units) * out_gain[...]).astype(jnp.bfloat16)
            change = dot(w_out[...], z)
            x = x + jnp.where(classes[r] > s, change, 0.0)
            held[r] = x.reshape(n, depth, quarter)
            return carry

        lax.fori_loop(0, SUBSTEPS, substep, 0)
        out[r, :, own] = held[r, me]
        for d in range(1, n):
            backward(r, d).start()
        return carry

    lax.fori_loop(0, rows, one_row, 0)

    for r in range(rows):
        for d in range(1, n):
            forward(r, d).wait_send()
            backward(r, d).wait()


def on_device(
    fields,
    zonal_courant,
    merid_courant,
    vert_courant,
    column_class,
    in_gain,
    w_in,
    w_up,
    w_down,
    out_gain,
    w_out,
):
    field_count, levels_here, rows_here, lon_count = fields.shape
    n = lax.axis_size("lev")
    lat_index = lax.axis_index("lat")
    lev_index = lax.axis_index("lev")
    row_start = lat_index * rows_here
    lev_start = lev_index * levels_here
    units = w_in.shape[1]
    inputs = w_in.shape[0]
    part = field_count * levels_here
    depth = -(-part // 16) * 16
    quarter = lon_count // n

    def by_source(array):
        tail = array.shape[1:]
        split = array.reshape((field_count, n, levels_here) + tail)
        split = jnp.moveaxis(split, 1, 0).reshape((n, part) + tail)
        split = jnp.pad(split, ((0, 0), (0, depth - part)) + ((0, 0),) * len(tail))
        return split.reshape((n * depth,) + tail)

    gain_in = by_source(in_gain[:, None])
    w_in_t = by_source(w_in).T
    w_out_t = by_source(w_out.T)
    w_up_t = w_up[0].T
    w_down_t = w_down[0].T
    own_class = lax.dynamic_slice(
        column_class, (row_start, lev_index * quarter), (rows_here, quarter)
    ).reshape(rows_here, 1, quarter)

    zonal, merid, vertical = face_winds(
        zonal_courant, merid_courant, vert_courant, 1, lev_start, row_start, levels_here, rows_here
    )
    state = fields
    for step in range(STEPS):
        extended = with_halo(state, (("lat", 2), ("lev", 1)), 1)
        state = transport(extended, zonal, merid, vertical)[:, 1:-1, 1:-1, :]
    by_row = state.reshape(part, rows_here, lon_count).transpose(1, 0, 2)
    by_row = jnp.pad(by_row, ((0, 0), (0, depth - part), (0, 0)))

    vmem = pl.BlockSpec(memory_space=pltpu.VMEM)
    done = pl.pallas_call(
        functools.partial(physics_kernel, n, inputs),
        out_shape=jax.ShapeDtypeStruct(by_row.shape, jnp.float32),
        in_specs=[vmem] * 8,
        out_specs=vmem,
        scratch_shapes=[
            pltpu.VMEM((rows_here, n, depth, quarter), jnp.float32),
            pltpu.SemaphoreType.DMA((rows_here, n - 1)),
            pltpu.SemaphoreType.DMA((rows_here, n - 1)),
            pltpu.SemaphoreType.DMA((rows_here, n - 1)),
            pltpu.SemaphoreType.DMA((rows_here, n - 1)),
        ],
        compiler_params=pltpu.CompilerParams(
            collective_id=0, has_side_effects=True, vmem_limit_bytes=48 * 2**20
        ),
    )(by_row, own_class, gain_in, w_in_t, w_up_t, w_down_t, out_gain[:, None], w_out_t)
    done = done[:, :part].transpose(1, 0, 2)
    return done.reshape(fields.shape)


def solution(mesh):
    return jax.shard_map(
        on_device,
        mesh=mesh,
        in_specs=(P(None, "lev", "lat", None), P(), P(), P(), P(), P(), P(), P(), P(), P(), P()),
        out_specs=P(None, "lev", "lat", None),
        check_vma=False,
    )
```

```python
import functools

import jax
import jax.numpy as jnp
from jax import lax
from jax.experimental import pallas as pl
from jax.experimental.pallas import tpu as pltpu
from jax.sharding import PartitionSpec as P

STEPS = 2
SUBSTEPS = 4
MESH = pl.DeviceIdType.MESH


def face_coefficients(zonal_courant, merid_courant, vert_courant, lev_start, row_start, levels, rows):
    east = lax.dynamic_slice(zonal_courant, (lev_start, row_start), (levels, rows))
    merid = jnp.pad(merid_courant, ((0, 0), (1, 1)))
    merid = lax.dynamic_slice(merid, (lev_start, row_start), (levels, rows + 1))
    vertical = jnp.pad(vert_courant, ((1, 1), (0, 0)))
    vertical = lax.dynamic_slice(vertical, (lev_start, row_start), (levels + 1, rows))
    south, north = merid[:, :-1], merid[:, 1:]
    above, below = vertical[:-1], vertical[1:]

    def plus(courant):
        return jnp.maximum(courant, 0.0)

    def minus(courant):
        return jnp.minimum(courant, 0.0)

    keep = 1.0 - (
        (plus(east) - minus(east)) + (plus(north) - minus(south)) + (plus(below) - minus(above))
    )
    parts = [
        keep, -minus(east), plus(east), -minus(north), plus(south), -minus(below), plus(above),
        jnp.zeros_like(keep),
    ]
    return jnp.stack(parts, axis=0).transpose(2, 1, 0)


def inverse_rms(values, entries):
    return lax.rsqrt(jnp.sum(values * values, axis=0, keepdims=True) / entries + 1e-06)


def dot(a, b):
    return jnp.dot(a, b, preferred_element_type=jnp.float32)


def column_kernel(
    n, lat_count, entries,
    fields, coefs, classes, in_gain, w_in, w_up, w_down, out_gain, w_out,
    result,
    raw, first, second, state, held, out, edge, lev_halo,
    load_sem, store_sem, lat_send, lat_recv, lev_send, lev_recv, fsend, frecv, bsend, brecv,
):
    me = lax.axis_index("lev")
    lat = lax.axis_index("lat")
    rows, field_count, slots, lons = state.shape
    levels = fields.shape[1]
    quarter = lons // n
    has_south, has_north = lat > 0, lat < lat_count - 1
    has_above, has_below = me > 0, me < n - 1

    def load(r):
        return pltpu.make_async_copy(
            fields.at[:, :, r, :], raw.at[r], load_sem.at[r]
        )

    def store(r):
        return pltpu.make_async_copy(
            raw.at[r], result.at[:, :, r, :], store_sem.at[r]
        )

    for r in range(rows):
        load(r).start()

    barrier = pltpu.get_barrier_semaphore()
    for d in range(1, n):
        pl.semaphore_signal(barrier, inc=1, device_id={"lev": lax.rem(me + d, n)}, device_id_type=MESH)

    @pl.when(has_south)
    def _():
        pl.semaphore_signal(barrier, inc=1, device_id={"lat": lat - 1}, device_id_type=MESH)

    @pl.when(has_north)
    def _():
        pl.semaphore_signal(barrier, inc=1, device_id={"lat": lat + 1}, device_id_type=MESH)

    south_count = (lat + lat_count - 1) // lat_count
    north_count = 1 - (lat + 1) // lat_count
    pl.semaphore_wait(barrier, n - 1 + south_count + north_count)

    slab = (field_count, slots, lons)

    @pl.when(jnp.logical_not(has_south))
    def _():
        first[0] = jnp.zeros(slab, jnp.float32)
        second[0] = jnp.zeros(slab, jnp.float32)

    @pl.when(jnp.logical_not(has_north))
    def _():
        first[rows + 1] = jnp.zeros(slab, jnp.float32)
        second[rows + 1] = jnp.zeros(slab, jnp.float32)

    edges = (rows, field_count, lons)

    @pl.when(jnp.logical_not(has_above))
    def _():
        lev_halo[0, 0] = jnp.zeros(edges, jnp.float32)
        lev_halo[1, 0] = jnp.zeros(edges, jnp.float32)

    @pl.when(jnp.logical_not(has_below))
    def _():
        lev_halo[0, 1] = jnp.zeros(edges, jnp.float32)
        lev_halo[1, 1] = jnp.zeros(edges, jnp.float32)

    def southward(step, cells):
        return pltpu.make_async_remote_copy(
            src_ref=cells.at[1], dst_ref=cells.at[rows + 1],
            send_sem=lat_send.at[step, 0], recv_sem=lat_recv.at[step, 0],
            device_id={"lat": lat - 1}, device_id_type=MESH,
        )

    def northward(step, cells):
        return pltpu.make_async_remote_copy(
            src_ref=cells.at[rows], dst_ref=cells.at[0],
            send_sem=lat_send.at[step, 1], recv_sem=lat_recv.at[step, 1],
            device_id={"lat": lat + 1}, device_id_type=MESH,
        )

    def upward(step):
        return pltpu.make_async_remote_copy(
            src_ref=edge.at[step, 0], dst_ref=lev_halo.at[step, 1],
            send_sem=lev_send.at[step, 0], recv_sem=lev_recv.at[step, 0],
            device_id={"lev": me - 1}, device_id_type=MESH,
        )

    def downward(step):
        return pltpu.make_async_remote_copy(
            src_ref=edge.at[step, 1], dst_ref=lev_halo.at[step, 0],
            send_sem=lev_send.at[step, 1], recv_sem=lev_recv.at[step, 1],
            device_id={"lev": me + 1}, device_id_type=MESH,
        )

    def when_all(pairs):
        for condition, act in pairs:
            pl.when(condition)(act)

    def send_lat(step, cells):
        when_all([
            (has_south, lambda: southward(step, cells).start()),
            (has_north, lambda: northward(step, cells).start()),
        ])

    def send_lev(step):
        when_all([
            (has_above, lambda: upward(step).start()),
            (has_below, lambda: downward(step).start()),
        ])

    def wait_lat(step, cells):
        when_all([
            (has_north, lambda: southward(step, cells).wait_recv()),
            (has_south, lambda: northward(step, cells).wait_recv()),
        ])

    def wait_lev(step):
        when_all([
            (has_below, lambda: upward(step).wait_recv()),
            (has_above, lambda: downward(step).wait_recv()),
        ])

    def finish_sends(step, cells):
        when_all([
            (has_south, lambda: southward(step, cells).wait_send()),
            (has_north, lambda: northward(step, cells).wait_send()),
            (has_above, lambda: upward(step).wait_send()),
            (has_below, lambda: downward(step).wait_send()),
        ])

    def take_edges(step, cells, r):
        for f in range(field_count):
            edge[step, 0, r, pl.ds(f, 1), :] = cells[r + 1, f, 0:1, :]
            edge[step, 1, r, pl.ds(f, 1), :] = cells[r + 1, f, levels - 1 : levels, :]

    level = lax.broadcasted_iota(jnp.int32, (slots, lons), 0)

    def advance(step, r, cells, store_row):
        block = coefs[r]
        keep, east, west, north, south, below, above = [block[:, i : i + 1] for i in range(7)]
        for f in range(field_count):
            q = cells[r + 1, f]
            q_below = jnp.where(
                level == levels - 1, lev_halo[step, 1, r, pl.ds(f, 1), :], pltpu.roll(q, slots - 1, 0)
            )
            q_above = jnp.where(
                level == 0, lev_halo[step, 0, r, pl.ds(f, 1), :], pltpu.roll(q, 1, 0)
            )
            new = keep * q + (east * pltpu.roll(q, lons - 1, 1) + west * pltpu.roll(q, 1, 1))
            new = new + (north * cells[r + 2, f] + south * cells[r, f])
            new = new + (below * q_below + above * q_above)
            store_row(f, jnp.where(level < levels, new, 0.0))

    for r in range(rows):
        load(r).wait()

    def gather_first(r, carry):
        for f in range(field_count):
            first[r + 1, f, 0:levels, :] = raw[r, f]
        take_edges(0, first, r)
        return carry

    lax.fori_loop(0, rows, gather_first, 0)
    send_lat(0, first)
    send_lev(0)
    wait_lev(0)
    wait_lat(0, first)

    def first_row(r, carry):
        def put(f, value):
            second[r + 1, f] = value

        advance(0, r, first, put)
        take_edges(1, second, r)
        return carry

    lax.fori_loop(0, rows, first_row, 0)
    send_lat(1, second)
    send_lev(1)
    wait_lev(1)
    wait_lat(1, second)

    own = pl.ds(pl.multiple_of(me * quarter, quarter), quarter)

    def forward(r, d):
        peer = lax.rem(me + d, n)
        there = pl.ds(pl.multiple_of(peer * quarter, quarter), quarter)
        return pltpu.make_async_remote_copy(
            src_ref=state.at[r, :, :, there],
            dst_ref=held.at[r, me],
            send_sem=fsend.at[r, d - 1],
            recv_sem=frecv.at[r, d - 1],
            device_id={"lev": peer},
            device_id_type=MESH,
        )

    def backward(r, d):
        peer = lax.rem(me + d, n)
        return pltpu.make_async_remote_copy(
            src_ref=held.at[r, peer],
            dst_ref=out.at[r, :, :, own],
            send_sem=bsend.at[r, d - 1],
            recv_sem=brecv.at[r, d - 1],
            device_id={"lev": peer},
            device_id_type=MESH,
        )

    def second_row(r, carry):
        def put(f, value):
            state[r, f] = value

        advance(1, r, second, put)
        for d in range(1, n):
            forward(r, d).start()
        return carry

    lax.fori_loop(0, rows, second_row, 0)

    def one_row(r, carry):
        held[r, me] = state[r, :, :, own]
        for d in range(1, n):
            forward(r, d).wait_recv()

        def substep(s, carry):
            x = held[r].reshape(n * field_count * slots, quarter)
            a = (x * inverse_rms(x, entries) * in_gain[...]).astype(jnp.bfloat16)
            h = dot(w_in[...], a)
            units = h.shape[0]
            g = (h * inverse_rms(h, units)).astype(jnp.bfloat16)
            v = dot(w_up[...], g)
            u = (v / (1.0 + jnp.exp(-v))).astype(jnp.bfloat16)
            h = h + dot(w_down[...], u)
            z = (h * inverse_rms(h, units) * out_gain[...]).astype(jnp.bfloat16)
            change = dot(w_out[...], z)
            x = x + jnp.where(classes[r] > s, change, 0.0)
            held[r] = x.reshape(n, field_count, slots, quarter)
            return carry

        lax.fori_loop(0, SUBSTEPS, substep, 0)
        out[r, :, :, own] = held[r, me]
        for d in range(1, n):
            backward(r, d).start()
        return carry

    lax.fori_loop(0, rows, one_row, 0)

    for r in range(rows):
        for d in range(1, n):
            backward(r, d).wait_recv()
        for f in range(field_count):
            raw[r, f] = out[r, f, 0:levels, :]
        store(r).start()
    for r in range(rows):
        for d in range(1, n):
            forward(r, d).wait_send()
            backward(r, d).wait_send()
    finish_sends(0, first)
    finish_sends(1, second)
    for r in range(rows):
        store(r).wait()


def on_device(
    fields,
    zonal_courant,
    merid_courant,
    vert_courant,
    column_class,
    in_gain,
    w_in,
    w_up,
    w_down,
    out_gain,
    w_out,
):
    field_count, levels_here, rows_here, lon_count = fields.shape
    n = lax.axis_size("lev")
    lat_index = lax.axis_index("lat")
    lev_index = lax.axis_index("lev")
    row_start = lat_index * rows_here
    lev_start = lev_index * levels_here
    inputs = w_in.shape[0]
    slots = -(-(levels_here + 1) // 16) * 16
    quarter = lon_count // n

    def by_source(array):
        tail = array.shape[1:]
        split = array.reshape((field_count, n, levels_here) + tail)
        split = jnp.moveaxis(split, 1, 0)
        split = jnp.pad(split, ((0, 0), (0, 0), (0, slots - levels_here)) + ((0, 0),) * len(tail))
        return split.reshape((n * field_count * slots,) + tail)

    gain_in = by_source(in_gain[:, None])
    w_in_t = by_source(w_in).T
    w_out_t = by_source(w_out.T)
    w_up_t = w_up[0].T
    w_down_t = w_down[0].T
    own_class = lax.dynamic_slice(
        column_class, (row_start, lev_index * quarter), (rows_here, quarter)
    ).reshape(rows_here, 1, quarter)
    coefs = face_coefficients(
        zonal_courant, merid_courant, vert_courant, lev_start, row_start, levels_here, rows_here
    )
    coefs = jnp.pad(coefs, ((0, 0), (0, slots - levels_here), (0, 0)))

    vmem = pl.BlockSpec(memory_space=pltpu.VMEM)
    hbm = pl.BlockSpec(memory_space=pl.ANY)
    pair = pltpu.SemaphoreType.DMA((STEPS, 2))
    grid = pltpu.SemaphoreType.DMA((rows_here, n - 1))
    single = pltpu.SemaphoreType.DMA((rows_here,))
    slab = (field_count, slots, lon_count)
    return pl.pallas_call(
        functools.partial(column_kernel, n, lax.axis_size("lat"), inputs),
        out_shape=jax.ShapeDtypeStruct(fields.shape, jnp.float32),
        in_specs=[hbm] + [vmem] * 8,
        out_specs=hbm,
        scratch_shapes=[
            pltpu.VMEM((rows_here, field_count, levels_here, lon_count), jnp.float32),
            pltpu.VMEM((rows_here + 2,) + slab, jnp.float32),
            pltpu.VMEM((rows_here + 2,) + slab, jnp.float32),
            pltpu.VMEM((rows_here,) + slab, jnp.float32),
            pltpu.VMEM((rows_here, n, field_count, slots, quarter), jnp.float32),
            pltpu.VMEM((rows_here,) + slab, jnp.float32),
            pltpu.VMEM((STEPS, 2, rows_here, field_count, lon_count), jnp.float32),
            pltpu.VMEM((STEPS, 2, rows_here, field_count, lon_count), jnp.float32),
            single, single, pair, pair, pair, pair, grid, grid, grid, grid,
        ],
        compiler_params=pltpu.CompilerParams(
            collective_id=0, has_side_effects=True, vmem_limit_bytes=48 * 2**20
        ),
    )(fields, coefs, own_class, gain_in, w_in_t, w_up_t, w_down_t, out_gain[:, None], w_out_t)


def solution(mesh):
    return jax.shard_map(
        on_device,
        mesh=mesh,
        in_specs=(P(None, "lev", "lat", None), P(), P(), P(), P(), P(), P(), P(), P(), P(), P()),
        out_specs=P(None, "lev", "lat", None),
        check_vma=False,
    )
```

```python
import functools

import jax
import jax.numpy as jnp
from jax import lax
from jax.experimental import pallas as pl
from jax.experimental.pallas import tpu as pltpu
from jax.sharding import PartitionSpec as P

STEPS = 2
SUBSTEPS = 4
MESH = pl.DeviceIdType.MESH


def face_coefficients(zonal_courant, merid_courant, vert_courant, lev_start, row_start, levels, rows):
    east = lax.dynamic_slice(zonal_courant, (lev_start, row_start), (levels, rows))
    merid = jnp.pad(merid_courant, ((0, 0), (1, 1)))
    merid = lax.dynamic_slice(merid, (lev_start, row_start), (levels, rows + 1))
    vertical = jnp.pad(vert_courant, ((1, 1), (0, 0)))
    vertical = lax.dynamic_slice(vertical, (lev_start, row_start), (levels + 1, rows))
    south, north = merid[:, :-1], merid[:, 1:]
    above, below = vertical[:-1], vertical[1:]

    def plus(courant):
        return jnp.maximum(courant, 0.0)

    def minus(courant):
        return jnp.minimum(courant, 0.0)

    keep = 1.0 - (
        (plus(east) - minus(east)) + (plus(north) - minus(south)) + (plus(below) - minus(above))
    )
    parts = [
        keep, -minus(east), plus(east), -minus(north), plus(south), -minus(below), plus(above),
        jnp.zeros_like(keep),
    ]
    return jnp.stack(parts, axis=0).transpose(2, 1, 0)


def inverse_rms(values, entries):
    return lax.rsqrt(jnp.sum(values * values, axis=0, keepdims=True) / entries + 1e-06)


def turn(source, target):
    width = 256

    def strip(i, carry):
        here = pl.ds(pl.multiple_of(i * width, width), width)
        target[:, here] = source[here, :].T
        return carry

    lax.fori_loop(0, source.shape[0] // width, strip, 0)


def dot(a, b):
    return jnp.dot(a, b, preferred_element_type=jnp.float32)


def column_kernel(
    n, lat_count, entries,
    fields, coefs, classes, in_gain, w_in, w_up, w_down, out_gain, w_out,
    result,
    up_t, down_t, raw, first, second, state, held, out, edge, lev_halo,
    load_sem, store_sem, lat_send, lat_recv, lev_send, lev_recv, fsend, frecv, bsend, brecv,
):
    me = lax.axis_index("lev")
    lat = lax.axis_index("lat")
    rows, field_count, slots, lons = state.shape
    levels = fields.shape[1]
    quarter = lons // n
    has_south, has_north = lat > 0, lat < lat_count - 1
    has_above, has_below = me > 0, me < n - 1

    def load(r):
        return pltpu.make_async_copy(
            fields.at[:, :, r, :], raw.at[r], load_sem.at[r]
        )

    def store(r):
        return pltpu.make_async_copy(
            raw.at[r], result.at[:, :, r, :], store_sem.at[r]
        )

    inner = range(1, rows - 1)
    for r in (0, rows - 1, *inner):
        load(r).start()

    barrier = pltpu.get_barrier_semaphore()
    for d in range(1, n):
        pl.semaphore_signal(barrier, inc=1, device_id={"lev": lax.rem(me + d, n)}, device_id_type=MESH)

    @pl.when(has_south)
    def _():
        pl.semaphore_signal(barrier, inc=1, device_id={"lat": lat - 1}, device_id_type=MESH)

    @pl.when(has_north)
    def _():
        pl.semaphore_signal(barrier, inc=1, device_id={"lat": lat + 1}, device_id_type=MESH)

    south_count = (lat + lat_count - 1) // lat_count
    north_count = 1 - (lat + 1) // lat_count
    pl.semaphore_wait(barrier, n - 1 + south_count + north_count)

    slab = (field_count, slots, lons)

    @pl.when(jnp.logical_not(has_south))
    def _():
        first[0] = jnp.zeros(slab, jnp.float32)
        second[0] = jnp.zeros(slab, jnp.float32)

    @pl.when(jnp.logical_not(has_north))
    def _():
        first[rows + 1] = jnp.zeros(slab, jnp.float32)
        second[rows + 1] = jnp.zeros(slab, jnp.float32)

    edges = (rows, field_count, lons)

    @pl.when(jnp.logical_not(has_above))
    def _():
        lev_halo[0, 0] = jnp.zeros(edges, jnp.float32)
        lev_halo[1, 0] = jnp.zeros(edges, jnp.float32)

    @pl.when(jnp.logical_not(has_below))
    def _():
        lev_halo[0, 1] = jnp.zeros(edges, jnp.float32)
        lev_halo[1, 1] = jnp.zeros(edges, jnp.float32)

    def southward(step, cells):
        return pltpu.make_async_remote_copy(
            src_ref=cells.at[1], dst_ref=cells.at[rows + 1],
            send_sem=lat_send.at[step, 0], recv_sem=lat_recv.at[step, 0],
            device_id={"lat": lat - 1}, device_id_type=MESH,
        )

    def northward(step, cells):
        return pltpu.make_async_remote_copy(
            src_ref=cells.at[rows], dst_ref=cells.at[0],
            send_sem=lat_send.at[step, 1], recv_sem=lat_recv.at[step, 1],
            device_id={"lat": lat + 1}, device_id_type=MESH,
        )

    def upward(step):
        return pltpu.make_async_remote_copy(
            src_ref=edge.at[step, 0], dst_ref=lev_halo.at[step, 1],
            send_sem=lev_send.at[step, 0], recv_sem=lev_recv.at[step, 0],
            device_id={"lev": me - 1}, device_id_type=MESH,
        )

    def downward(step):
        return pltpu.make_async_remote_copy(
            src_ref=edge.at[step, 1], dst_ref=lev_halo.at[step, 0],
            send_sem=lev_send.at[step, 1], recv_sem=lev_recv.at[step, 1],
            device_id={"lev": me + 1}, device_id_type=MESH,
        )

    def when_all(pairs):
        for condition, act in pairs:
            pl.when(condition)(act)

    def send_lat(step, cells):
        when_all([
            (has_south, lambda: southward(step, cells).start()),
            (has_north, lambda: northward(step, cells).start()),
        ])

    def send_lev(step):
        when_all([
            (has_above, lambda: upward(step).start()),
            (has_below, lambda: downward(step).start()),
        ])

    def wait_lat(step, cells):
        when_all([
            (has_north, lambda: southward(step, cells).wait_recv()),
            (has_south, lambda: northward(step, cells).wait_recv()),
        ])

    def wait_lev(step):
        when_all([
            (has_below, lambda: upward(step).wait_recv()),
            (has_above, lambda: downward(step).wait_recv()),
        ])

    def finish_sends(step, cells):
        when_all([
            (has_south, lambda: southward(step, cells).wait_send()),
            (has_north, lambda: northward(step, cells).wait_send()),
            (has_above, lambda: upward(step).wait_send()),
            (has_below, lambda: downward(step).wait_send()),
        ])

    def take_edges(step, cells, r):
        for f in range(field_count):
            edge[step, 0, r, pl.ds(f, 1), :] = cells[r + 1, f, 0:1, :]
            edge[step, 1, r, pl.ds(f, 1), :] = cells[r + 1, f, levels - 1 : levels, :]

    level = lax.broadcasted_iota(jnp.int32, (slots, lons), 0)

    def advance(step, r, cells, store_row):
        block = coefs[r]
        keep, east, west, north, south, below, above = [block[:, i : i + 1] for i in range(7)]
        for f in range(field_count):
            q = cells[r + 1, f]
            q_below = jnp.where(
                level == levels - 1, lev_halo[step, 1, r, pl.ds(f, 1), :], pltpu.roll(q, slots - 1, 0)
            )
            q_above = jnp.where(
                level == 0, lev_halo[step, 0, r, pl.ds(f, 1), :], pltpu.roll(q, 1, 0)
            )
            new = keep * q + (east * pltpu.roll(q, lons - 1, 1) + west * pltpu.roll(q, 1, 1))
            new = new + (north * cells[r + 2, f] + south * cells[r, f])
            new = new + (below * q_below + above * q_above)
            store_row(f, jnp.where(level < levels, new, 0.0))

    def gather_first(r):
        load(r).wait()
        for f in range(field_count):
            first[r + 1, f, 0:levels, :] = raw[r, f]
        take_edges(0, first, r)

    def outer_rows(act):
        def body(i, carry):
            act(i * (rows - 1))
            return carry

        lax.fori_loop(0, 2, body, 0)

    def inner_rows(act):
        def body(r, carry):
            act(r)
            return carry

        lax.fori_loop(1, rows - 1, body, 0)

    outer_rows(gather_first)
    send_lat(0, first)
    inner_rows(gather_first)
    send_lev(0)
    wait_lev(0)
    wait_lat(0, first)

    def first_row(r):
        def put(f, value):
            second[r + 1, f] = value

        advance(0, r, first, put)
        take_edges(1, second, r)

    outer_rows(first_row)
    send_lat(1, second)
    inner_rows(first_row)
    send_lev(1)
    wait_lev(1)

    own = pl.ds(pl.multiple_of(me * quarter, quarter), quarter)

    def forward(r, d):
        peer = lax.rem(me + d, n)
        there = pl.ds(pl.multiple_of(peer * quarter, quarter), quarter)
        return pltpu.make_async_remote_copy(
            src_ref=state.at[r, :, :, there],
            dst_ref=held.at[r, me],
            send_sem=fsend.at[r, d - 1],
            recv_sem=frecv.at[r, d - 1],
            device_id={"lev": peer},
            device_id_type=MESH,
        )

    def backward(r, d):
        peer = lax.rem(me + d, n)
        return pltpu.make_async_remote_copy(
            src_ref=held.at[r, peer],
            dst_ref=out.at[r, :, :, own],
            send_sem=bsend.at[r, d - 1],
            recv_sem=brecv.at[r, d - 1],
            device_id={"lev": peer},
            device_id_type=MESH,
        )

    def second_row(r):
        def put(f, value):
            state[r, f] = value

        advance(1, r, second, put)

    def send_forward(r):
        for d in range(1, n):
            forward(r, d).start()

    def second_and_send(r):
        second_row(r)
        send_forward(r)

    inner_rows(second_and_send)
    wait_lat(1, second)
    outer_rows(second_row)
    turn(w_up, up_t)
    turn(w_down, down_t)

    def one_row(i, carry):
        r = (i + 1) % (rows - 1) + (i // (rows - 1)) * (rows - 2)
        held[r, me] = state[r, :, :, own]
        for d in range(1, n):
            forward(r, d).wait_recv()

        @pl.when(i == 0)
        def _():
            outer_rows(send_forward)

        def substep(s, carry):
            x = held[r].reshape(n * field_count * slots, quarter)
            a = (x * inverse_rms(x, entries) * in_gain[...]).astype(jnp.bfloat16)
            h = dot(w_in[...], a)
            units = h.shape[0]
            g = (h * inverse_rms(h, units)).astype(jnp.bfloat16)
            v = dot(up_t[...], g)
            u = (v / (1.0 + jnp.exp(-v))).astype(jnp.bfloat16)
            h = h + dot(down_t[...], u)
            z = (h * inverse_rms(h, units) * out_gain[...]).astype(jnp.bfloat16)
            change = dot(w_out[...], z)
            x = x + jnp.where(classes[r] > s, change, 0.0)
            held[r] = x.reshape(n, field_count, slots, quarter)
            return carry

        lax.fori_loop(0, SUBSTEPS, substep, 0)
        out[r, :, :, own] = held[r, me]
        for d in range(1, n):
            backward(r, d).start()
        return carry

    lax.fori_loop(0, rows, one_row, 0)

    for r in (*inner, 0, rows - 1):
        for d in range(1, n):
            backward(r, d).wait_recv()
        for f in range(field_count):
            raw[r, f] = out[r, f, 0:levels, :]
        store(r).start()
    for r in range(rows):
        for d in range(1, n):
            forward(r, d).wait_send()
            backward(r, d).wait_send()
    finish_sends(0, first)
    finish_sends(1, second)
    for r in range(rows):
        store(r).wait()


def on_device(
    fields,
    zonal_courant,
    merid_courant,
    vert_courant,
    column_class,
    in_gain,
    w_in,
    w_up,
    w_down,
    out_gain,
    w_out,
):
    field_count, levels_here, rows_here, lon_count = fields.shape
    n = lax.axis_size("lev")
    lat_index = lax.axis_index("lat")
    lev_index = lax.axis_index("lev")
    row_start = lat_index * rows_here
    lev_start = lev_index * levels_here
    inputs = w_in.shape[0]
    slots = -(-(levels_here + 1) // 16) * 16
    quarter = lon_count // n

    def by_source(array):
        tail = array.shape[1:]
        split = array.reshape((field_count, n, levels_here) + tail)
        split = jnp.moveaxis(split, 1, 0)
        split = jnp.pad(split, ((0, 0), (0, 0), (0, slots - levels_here)) + ((0, 0),) * len(tail))
        return split.reshape((n * field_count * slots,) + tail)

    gain_in = by_source(in_gain[:, None])
    w_in_t = by_source(w_in).T
    w_out_t = by_source(w_out.T)
    own_class = lax.dynamic_slice(
        column_class, (row_start, lev_index * quarter), (rows_here, quarter)
    ).reshape(rows_here, 1, quarter)
    coefs = face_coefficients(
        zonal_courant, merid_courant, vert_courant, lev_start, row_start, levels_here, rows_here
    )
    coefs = jnp.pad(coefs, ((0, 0), (0, slots - levels_here), (0, 0)))

    vmem = pl.BlockSpec(memory_space=pltpu.VMEM)
    hbm = pl.BlockSpec(memory_space=pl.ANY)
    pair = pltpu.SemaphoreType.DMA((STEPS, 2))
    grid = pltpu.SemaphoreType.DMA((rows_here, n - 1))
    single = pltpu.SemaphoreType.DMA((rows_here,))
    slab = (field_count, slots, lon_count)
    return pl.pallas_call(
        functools.partial(column_kernel, n, lax.axis_size("lat"), inputs),
        out_shape=jax.ShapeDtypeStruct(fields.shape, jnp.float32),
        in_specs=[hbm] + [vmem] * 8,
        out_specs=hbm,
        scratch_shapes=[
            pltpu.VMEM(w_up.shape[1:], w_up.dtype),
            pltpu.VMEM(w_down.shape[1:], w_down.dtype),
            pltpu.VMEM((rows_here, field_count, levels_here, lon_count), jnp.float32),
            pltpu.VMEM((rows_here + 2,) + slab, jnp.float32),
            pltpu.VMEM((rows_here + 2,) + slab, jnp.float32),
            pltpu.VMEM((rows_here,) + slab, jnp.float32),
            pltpu.VMEM((rows_here, n, field_count, slots, quarter), jnp.float32),
            pltpu.VMEM((rows_here,) + slab, jnp.float32),
            pltpu.VMEM((STEPS, 2, rows_here, field_count, lon_count), jnp.float32),
            pltpu.VMEM((STEPS, 2, rows_here, field_count, lon_count), jnp.float32),
            single, single, pair, pair, pair, pair, grid, grid, grid, grid,
        ],
        compiler_params=pltpu.CompilerParams(
            collective_id=0, has_side_effects=True, vmem_limit_bytes=48 * 2**20
        ),
    )(fields, coefs, own_class, gain_in, w_in_t, w_up[0], w_down[0], out_gain[:, None], w_out_t)


def solution(mesh):
    return jax.shard_map(
        on_device,
        mesh=mesh,
        in_specs=(P(None, "lev", "lat", None), P(), P(), P(), P(), P(), P(), P(), P(), P(), P()),
        out_specs=P(None, "lev", "lat", None),
        check_vma=False,
    )
```

```python
import functools

import jax
import jax.numpy as jnp
from jax import lax
from jax.experimental import pallas as pl
from jax.experimental.pallas import tpu as pltpu
from jax.sharding import PartitionSpec as P

STEPS = 2
SUBSTEPS = 4
MESH = pl.DeviceIdType.MESH


def face_coefficients(zonal_courant, merid_courant, vert_courant, lev_start, row_start, levels, rows):
    east = lax.dynamic_slice(zonal_courant, (lev_start, row_start), (levels, rows))
    merid = jnp.pad(merid_courant, ((0, 0), (1, 1)))
    merid = lax.dynamic_slice(merid, (lev_start, row_start), (levels, rows + 1))
    vertical = jnp.pad(vert_courant, ((1, 1), (0, 0)))
    vertical = lax.dynamic_slice(vertical, (lev_start, row_start), (levels + 1, rows))
    south, north = merid[:, :-1], merid[:, 1:]
    above, below = vertical[:-1], vertical[1:]

    def plus(courant):
        return jnp.maximum(courant, 0.0)

    def minus(courant):
        return jnp.minimum(courant, 0.0)

    keep = 1.0 - (
        (plus(east) - minus(east)) + (plus(north) - minus(south)) + (plus(below) - minus(above))
    )
    parts = [
        keep, -minus(east), plus(east), -minus(north), plus(south), -minus(below), plus(above),
        jnp.zeros_like(keep),
    ]
    return jnp.stack(parts, axis=0).transpose(2, 1, 0)


def inverse_rms(values, entries):
    return lax.rsqrt(jnp.sum(values * values, axis=0, keepdims=True) / entries + 1e-06)


def turn(source, target):
    width = 256

    def strip(i, carry):
        here = pl.ds(pl.multiple_of(i * width, width), width)
        target[:, here] = source[here, :].T
        return carry

    lax.fori_loop(0, source.shape[0] // width, strip, 0)


def dot(a, b):
    return jnp.dot(a, b, preferred_element_type=jnp.float32)


def column_kernel(
    n, lat_count, entries,
    fields, coefs, classes, in_gain, w_in, w_up, w_down, out_gain, w_out,
    result,
    column, up_t, down_t, raw, first, second, state, held, out, edge, lev_halo,
    load_sem, store_sem, lat_send, lat_recv, lev_send, lev_recv, fsend, frecv, bsend, brecv,
):
    me = lax.axis_index("lev")
    lat = lax.axis_index("lat")
    rows, field_count, levels, lons = state.shape
    slots = first.shape[2]
    quarter = lons // n
    has_south, has_north = lat > 0, lat < lat_count - 1
    has_above, has_below = me > 0, me < n - 1

    def load(r):
        return pltpu.make_async_copy(
            fields.at[:, :, r, :], raw.at[r], load_sem.at[r]
        )

    def store(r):
        return pltpu.make_async_copy(
            out.at[r], result.at[:, :, r, :], store_sem.at[r]
        )

    inner = range(1, rows - 1)
    for r in (0, rows - 1, *inner):
        load(r).start()

    barrier = pltpu.get_barrier_semaphore()
    for d in range(1, n):
        pl.semaphore_signal(barrier, inc=1, device_id={"lev": lax.rem(me + d, n)}, device_id_type=MESH)

    @pl.when(has_south)
    def _():
        pl.semaphore_signal(barrier, inc=1, device_id={"lat": lat - 1}, device_id_type=MESH)

    @pl.when(has_north)
    def _():
        pl.semaphore_signal(barrier, inc=1, device_id={"lat": lat + 1}, device_id_type=MESH)

    south_count = (lat + lat_count - 1) // lat_count
    north_count = 1 - (lat + 1) // lat_count
    pl.semaphore_wait(barrier, n - 1 + south_count + north_count)

    slab = (field_count, slots, lons)

    @pl.when(jnp.logical_not(has_south))
    def _():
        first[0] = jnp.zeros(slab, jnp.float32)
        second[0] = jnp.zeros(slab, jnp.float32)

    @pl.when(jnp.logical_not(has_north))
    def _():
        first[rows + 1] = jnp.zeros(slab, jnp.float32)
        second[rows + 1] = jnp.zeros(slab, jnp.float32)

    edges = (rows, field_count, lons)

    @pl.when(jnp.logical_not(has_above))
    def _():
        lev_halo[0, 0] = jnp.zeros(edges, jnp.float32)
        lev_halo[1, 0] = jnp.zeros(edges, jnp.float32)

    @pl.when(jnp.logical_not(has_below))
    def _():
        lev_halo[0, 1] = jnp.zeros(edges, jnp.float32)
        lev_halo[1, 1] = jnp.zeros(edges, jnp.float32)

    def southward(step, cells):
        return pltpu.make_async_remote_copy(
            src_ref=cells.at[1], dst_ref=cells.at[rows + 1],
            send_sem=lat_send.at[step, 0], recv_sem=lat_recv.at[step, 0],
            device_id={"lat": lat - 1}, device_id_type=MESH,
        )

    def northward(step, cells):
        return pltpu.make_async_remote_copy(
            src_ref=cells.at[rows], dst_ref=cells.at[0],
            send_sem=lat_send.at[step, 1], recv_sem=lat_recv.at[step, 1],
            device_id={"lat": lat + 1}, device_id_type=MESH,
        )

    def upward(step):
        return pltpu.make_async_remote_copy(
            src_ref=edge.at[step, 0], dst_ref=lev_halo.at[step, 1],
            send_sem=lev_send.at[step, 0], recv_sem=lev_recv.at[step, 0],
            device_id={"lev": me - 1}, device_id_type=MESH,
        )

    def downward(step):
        return pltpu.make_async_remote_copy(
            src_ref=edge.at[step, 1], dst_ref=lev_halo.at[step, 0],
            send_sem=lev_send.at[step, 1], recv_sem=lev_recv.at[step, 1],
            device_id={"lev": me + 1}, device_id_type=MESH,
        )

    def when_all(pairs):
        for condition, act in pairs:
            pl.when(condition)(act)

    def send_lat(step, cells):
        when_all([
            (has_south, lambda: southward(step, cells).start()),
            (has_north, lambda: northward(step, cells).start()),
        ])

    def send_lev(step):
        when_all([
            (has_above, lambda: upward(step).start()),
            (has_below, lambda: downward(step).start()),
        ])

    def wait_lat(step, cells):
        when_all([
            (has_north, lambda: southward(step, cells).wait_recv()),
            (has_south, lambda: northward(step, cells).wait_recv()),
        ])

    def wait_lev(step):
        when_all([
            (has_below, lambda: upward(step).wait_recv()),
            (has_above, lambda: downward(step).wait_recv()),
        ])

    def finish_sends(step, cells):
        when_all([
            (has_south, lambda: southward(step, cells).wait_send()),
            (has_north, lambda: northward(step, cells).wait_send()),
            (has_above, lambda: upward(step).wait_send()),
            (has_below, lambda: downward(step).wait_send()),
        ])

    def take_edges(step, cells, r):
        for f in range(field_count):
            edge[step, 0, r, pl.ds(f, 1), :] = cells[r + 1, f, 0:1, :]
            edge[step, 1, r, pl.ds(f, 1), :] = cells[r + 1, f, levels - 1 : levels, :]

    level = lax.broadcasted_iota(jnp.int32, (slots, lons), 0)

    def advance(step, r, cells, store_row):
        block = coefs[r]
        keep, east, west, north, south, below, above = [block[:, i : i + 1] for i in range(7)]
        for f in range(field_count):
            q = cells[r + 1, f]
            q_below = jnp.where(
                level == levels - 1, lev_halo[step, 1, r, pl.ds(f, 1), :], pltpu.roll(q, slots - 1, 0)
            )
            q_above = jnp.where(
                level == 0, lev_halo[step, 0, r, pl.ds(f, 1), :], pltpu.roll(q, 1, 0)
            )
            new = keep * q + (east * pltpu.roll(q, lons - 1, 1) + west * pltpu.roll(q, 1, 1))
            new = new + (north * cells[r + 2, f] + south * cells[r, f])
            new = new + (below * q_below + above * q_above)
            store_row(f, new)

    def gather_first(r):
        load(r).wait()
        for f in range(field_count):
            first[r + 1, f, 0:levels, :] = raw[r, f]
        take_edges(0, first, r)

    def outer_rows(act):
        def body(i, carry):
            act(i * (rows - 1))
            return carry

        lax.fori_loop(0, 2, body, 0)

    def inner_rows(act):
        def body(r, carry):
            act(r)
            return carry

        lax.fori_loop(1, rows - 1, body, 0)

    outer_rows(gather_first)
    send_lat(0, first)
    inner_rows(gather_first)
    send_lev(0)
    wait_lev(0)
    wait_lat(0, first)

    def first_row(r):
        def put(f, value):
            second[r + 1, f] = value

        advance(0, r, first, put)
        take_edges(1, second, r)

    outer_rows(first_row)
    send_lat(1, second)
    inner_rows(first_row)
    send_lev(1)
    wait_lev(1)

    own = pl.ds(pl.multiple_of(me * quarter, quarter), quarter)

    def forward(r, d):
        peer = lax.rem(me + d, n)
        there = pl.ds(pl.multiple_of(peer * quarter, quarter), quarter)
        return pltpu.make_async_remote_copy(
            src_ref=state.at[r, :, :, there],
            dst_ref=held.at[r, me],
            send_sem=fsend.at[r, d - 1],
            recv_sem=frecv.at[r, d - 1],
            device_id={"lev": peer},
            device_id_type=MESH,
        )

    def backward(r, d):
        peer = lax.rem(me + d, n)
        return pltpu.make_async_remote_copy(
            src_ref=held.at[r, peer],
            dst_ref=out.at[r, :, :, own],
            send_sem=bsend.at[r, d - 1],
            recv_sem=brecv.at[r, d - 1],
            device_id={"lev": peer},
            device_id_type=MESH,
        )

    def second_row(r):
        def put(f, value):
            state[r, f] = value[:levels]

        advance(1, r, second, put)

    def send_forward(r):
        for d in range(1, n):
            forward(r, d).start()

    def second_and_send(r):
        second_row(r)
        send_forward(r)

    inner_rows(second_and_send)
    wait_lat(1, second)
    outer_rows(second_row)
    column[...] = jnp.zeros(column.shape, jnp.float32)
    turn(w_up, up_t)
    turn(w_down, down_t)

    def one_row(i, carry):
        r = (i + 1) % (rows - 1) + (i // (rows - 1)) * (rows - 2)
        held[r, me] = state[r, :, :, own]
        for d in range(1, n):
            forward(r, d).wait_recv()

        @pl.when(i == 0)
        def _():
            outer_rows(send_forward)

        def substep(s, carry):
            x = column[...].reshape(n * field_count * slots, quarter)
            a = (x * inverse_rms(x, entries) * in_gain[...]).astype(jnp.bfloat16)
            h = dot(w_in[...], a)
            units = h.shape[0]
            g = (h * inverse_rms(h, units)).astype(jnp.bfloat16)
            v = dot(up_t[...], g)
            u = (v / (1.0 + jnp.exp(-v))).astype(jnp.bfloat16)
            h = h + dot(down_t[...], u)
            z = (h * inverse_rms(h, units) * out_gain[...]).astype(jnp.bfloat16)
            change = dot(w_out[...], z)
            x = x + jnp.where(classes[r] > s, change, 0.0)
            column[...] = x.reshape(n, field_count, slots, quarter)
            return carry

        for p in range(n):
            for f in range(field_count):
                column[p, f, 0:levels, :] = held[r, p, f]
        lax.fori_loop(0, SUBSTEPS, substep, 0)
        for p in range(n):
            for f in range(field_count):
                held[r, p, f] = column[p, f, 0:levels, :]
        out[r, :, :, own] = held[r, me]
        for d in range(1, n):
            backward(r, d).start()
        return carry

    lax.fori_loop(0, rows, one_row, 0)

    for r in (*inner, 0, rows - 1):
        for d in range(1, n):
            backward(r, d).wait_recv()
        store(r).start()
    for r in range(rows):
        for d in range(1, n):
            forward(r, d).wait_send()
            backward(r, d).wait_send()
    finish_sends(0, first)
    finish_sends(1, second)
    for r in range(rows):
        store(r).wait()


def on_device(
    fields,
    zonal_courant,
    merid_courant,
    vert_courant,
    column_class,
    in_gain,
    w_in,
    w_up,
    w_down,
    out_gain,
    w_out,
):
    field_count, levels_here, rows_here, lon_count = fields.shape
    n = lax.axis_size("lev")
    lat_index = lax.axis_index("lat")
    lev_index = lax.axis_index("lev")
    row_start = lat_index * rows_here
    lev_start = lev_index * levels_here
    inputs = w_in.shape[0]
    slots = -(-(levels_here + 1) // 16) * 16
    quarter = lon_count // n

    def by_source(array):
        tail = array.shape[1:]
        split = array.reshape((field_count, n, levels_here) + tail)
        split = jnp.moveaxis(split, 1, 0)
        split = jnp.pad(split, ((0, 0), (0, 0), (0, slots - levels_here)) + ((0, 0),) * len(tail))
        return split.reshape((n * field_count * slots,) + tail)

    gain_in = by_source(in_gain[:, None])
    w_in_t = by_source(w_in).T
    w_out_t = by_source(w_out.T)
    own_class = lax.dynamic_slice(
        column_class, (row_start, lev_index * quarter), (rows_here, quarter)
    ).reshape(rows_here, 1, quarter)
    coefs = face_coefficients(
        zonal_courant, merid_courant, vert_courant, lev_start, row_start, levels_here, rows_here
    )
    coefs = jnp.pad(coefs, ((0, 0), (0, slots - levels_here), (0, 0)))

    vmem = pl.BlockSpec(memory_space=pltpu.VMEM)
    hbm = pl.BlockSpec(memory_space=pl.ANY)
    pair = pltpu.SemaphoreType.DMA((STEPS, 2))
    grid = pltpu.SemaphoreType.DMA((rows_here, n - 1))
    single = pltpu.SemaphoreType.DMA((rows_here,))
    slab = (field_count, slots, lon_count)
    return pl.pallas_call(
        functools.partial(column_kernel, n, lax.axis_size("lat"), inputs),
        out_shape=jax.ShapeDtypeStruct(fields.shape, jnp.float32),
        in_specs=[hbm] + [vmem] * 8,
        out_specs=hbm,
        scratch_shapes=[
            pltpu.VMEM((n, field_count, slots, quarter), jnp.float32),
            pltpu.VMEM(w_up.shape[1:], w_up.dtype),
            pltpu.VMEM(w_down.shape[1:], w_down.dtype),
            pltpu.VMEM((rows_here, field_count, levels_here, lon_count), jnp.float32),
            pltpu.VMEM((rows_here + 2,) + slab, jnp.float32),
            pltpu.VMEM((rows_here + 2,) + slab, jnp.float32),
            pltpu.VMEM((rows_here, field_count, levels_here, lon_count), jnp.float32),
            pltpu.VMEM((rows_here, n, field_count, levels_here, quarter), jnp.float32),
            pltpu.VMEM((rows_here, field_count, levels_here, lon_count), jnp.float32),
            pltpu.VMEM((STEPS, 2, rows_here, field_count, lon_count), jnp.float32),
            pltpu.VMEM((STEPS, 2, rows_here, field_count, lon_count), jnp.float32),
            single, single, pair, pair, pair, pair, grid, grid, grid, grid,
        ],
        compiler_params=pltpu.CompilerParams(
            collective_id=0, has_side_effects=True, vmem_limit_bytes=48 * 2**20
        ),
    )(fields, coefs, own_class, gain_in, w_in_t, w_up[0], w_down[0], out_gain[:, None], w_out_t)


def solution(mesh):
    return jax.shard_map(
        on_device,
        mesh=mesh,
        in_specs=(P(None, "lev", "lat", None), P(), P(), P(), P(), P(), P(), P(), P(), P(), P()),
        out_specs=P(None, "lev", "lat", None),
        check_vma=False,
    )
```

```python
import functools

import jax
import jax.numpy as jnp
from jax import lax
from jax.experimental import pallas as pl
from jax.experimental.pallas import tpu as pltpu
from jax.sharding import PartitionSpec as P

STEPS = 2
SUBSTEPS = 4
MESH = pl.DeviceIdType.MESH


def face_coefficients(zonal_courant, merid_courant, vert_courant, lev_start, row_start, levels, rows):
    east = lax.dynamic_slice(zonal_courant, (lev_start, row_start), (levels, rows))
    merid = jnp.pad(merid_courant, ((0, 0), (1, 1)))
    merid = lax.dynamic_slice(merid, (lev_start, row_start), (levels, rows + 1))
    vertical = jnp.pad(vert_courant, ((1, 1), (0, 0)))
    vertical = lax.dynamic_slice(vertical, (lev_start, row_start), (levels + 1, rows))
    south, north = merid[:, :-1], merid[:, 1:]
    above, below = vertical[:-1], vertical[1:]

    def plus(courant):
        return jnp.maximum(courant, 0.0)

    def minus(courant):
        return jnp.minimum(courant, 0.0)

    keep = 1.0 - (
        (plus(east) - minus(east)) + (plus(north) - minus(south)) + (plus(below) - minus(above))
    )
    parts = [
        keep, -minus(east), plus(east), -minus(north), plus(south), -minus(below), plus(above),
        jnp.zeros_like(keep),
    ]
    return jnp.stack(parts, axis=0).transpose(2, 1, 0)


def inverse_rms(values, entries):
    return lax.rsqrt(jnp.sum(values * values, axis=0, keepdims=True) / entries + 1e-06)


def turn(source, target):
    width = 256

    def strip(i, carry):
        here = pl.ds(pl.multiple_of(i * width, width), width)
        target[:, here] = source[here, :].T
        return carry

    lax.fori_loop(0, source.shape[0] // width, strip, 0)


def dot(a, b):
    return jnp.dot(a, b, preferred_element_type=jnp.float32)


def column_kernel(
    n, lat_count, entries,
    fields, coefs, classes, in_gain, w_in, w_up, w_down, out_gain, w_out,
    result,
    column, up_t, down_t, raw, first, second, state, held, out, edge, lev_halo,
    load_sem, store_sem, lat_send, lat_recv, lev_send, lev_recv, fsend, frecv, bsend, brecv,
):
    me = lax.axis_index("lev")
    lat = lax.axis_index("lat")
    rows, field_count, levels, lons = state.shape
    slots = first.shape[2]
    quarter = lons // n
    has_south, has_north = lat > 0, lat < lat_count - 1
    has_above, has_below = me > 0, me < n - 1

    def load(r):
        return pltpu.make_async_copy(
            fields.at[:, :, r, :], raw.at[r], load_sem.at[r]
        )

    def store(r):
        return pltpu.make_async_copy(
            out.at[r], result.at[:, :, r, :], store_sem.at[r]
        )

    inner = range(1, rows - 1)
    for r in (0, rows - 1, *inner):
        load(r).start()

    barrier = pltpu.get_barrier_semaphore()
    for d in range(1, n):
        pl.semaphore_signal(barrier, inc=1, device_id={"lev": lax.rem(me + d, n)}, device_id_type=MESH)

    @pl.when(has_south)
    def _():
        pl.semaphore_signal(barrier, inc=1, device_id={"lat": lat - 1}, device_id_type=MESH)

    @pl.when(has_north)
    def _():
        pl.semaphore_signal(barrier, inc=1, device_id={"lat": lat + 1}, device_id_type=MESH)

    south_count = (lat + lat_count - 1) // lat_count
    north_count = 1 - (lat + 1) // lat_count
    pl.semaphore_wait(barrier, n - 1 + south_count + north_count)

    slab = (field_count, slots, lons)

    @pl.when(jnp.logical_not(has_south))
    def _():
        first[0] = jnp.zeros(slab, jnp.float32)
        second[0] = jnp.zeros(slab, jnp.float32)

    @pl.when(jnp.logical_not(has_north))
    def _():
        first[rows + 1] = jnp.zeros(slab, jnp.float32)
        second[rows + 1] = jnp.zeros(slab, jnp.float32)

    edges = (rows, field_count, lons)

    @pl.when(jnp.logical_not(has_above))
    def _():
        lev_halo[0, 0] = jnp.zeros(edges, jnp.float32)
        lev_halo[1, 0] = jnp.zeros(edges, jnp.float32)

    @pl.when(jnp.logical_not(has_below))
    def _():
        lev_halo[0, 1] = jnp.zeros(edges, jnp.float32)
        lev_halo[1, 1] = jnp.zeros(edges, jnp.float32)

    def southward(step, cells):
        return pltpu.make_async_remote_copy(
            src_ref=cells.at[1], dst_ref=cells.at[rows + 1],
            send_sem=lat_send.at[step, 0], recv_sem=lat_recv.at[step, 0],
            device_id={"lat": lat - 1}, device_id_type=MESH,
        )

    def northward(step, cells):
        return pltpu.make_async_remote_copy(
            src_ref=cells.at[rows], dst_ref=cells.at[0],
            send_sem=lat_send.at[step, 1], recv_sem=lat_recv.at[step, 1],
            device_id={"lat": lat + 1}, device_id_type=MESH,
        )

    def upward(step):
        return pltpu.make_async_remote_copy(
            src_ref=edge.at[step, 0], dst_ref=lev_halo.at[step, 1],
            send_sem=lev_send.at[step, 0], recv_sem=lev_recv.at[step, 0],
            device_id={"lev": me - 1}, device_id_type=MESH,
        )

    def downward(step):
        return pltpu.make_async_remote_copy(
            src_ref=edge.at[step, 1], dst_ref=lev_halo.at[step, 0],
            send_sem=lev_send.at[step, 1], recv_sem=lev_recv.at[step, 1],
            device_id={"lev": me + 1}, device_id_type=MESH,
        )

    def when_all(pairs):
        for condition, act in pairs:
            pl.when(condition)(act)

    def send_lat(step, cells):
        when_all([
            (has_south, lambda: southward(step, cells).start()),
            (has_north, lambda: northward(step, cells).start()),
        ])

    def send_lev(step):
        when_all([
            (has_above, lambda: upward(step).start()),
            (has_below, lambda: downward(step).start()),
        ])

    def wait_lat(step, cells):
        when_all([
            (has_north, lambda: southward(step, cells).wait_recv()),
            (has_south, lambda: northward(step, cells).wait_recv()),
        ])

    def wait_lev(step):
        when_all([
            (has_below, lambda: upward(step).wait_recv()),
            (has_above, lambda: downward(step).wait_recv()),
        ])

    def finish_sends(step, cells):
        when_all([
            (has_south, lambda: southward(step, cells).wait_send()),
            (has_north, lambda: northward(step, cells).wait_send()),
            (has_above, lambda: upward(step).wait_send()),
            (has_below, lambda: downward(step).wait_send()),
        ])

    def take_edges(step, cells, r):
        for f in range(field_count):
            edge[step, 0, r, pl.ds(f, 1), :] = cells[r + 1, f, 0:1, :]
            edge[step, 1, r, pl.ds(f, 1), :] = cells[r + 1, f, levels - 1 : levels, :]

    level = lax.broadcasted_iota(jnp.int32, (slots, lons), 0)

    def advance(step, r, cells, store_row):
        block = coefs[r]
        keep, east, west, north, south, below, above = [block[:, i : i + 1] for i in range(7)]
        for f in range(field_count):
            q = cells[r + 1, f]
            q_below = jnp.where(
                level == levels - 1, lev_halo[step, 1, r, pl.ds(f, 1), :], pltpu.roll(q, slots - 1, 0)
            )
            q_above = jnp.where(
                level == 0, lev_halo[step, 0, r, pl.ds(f, 1), :], pltpu.roll(q, 1, 0)
            )
            new = keep * q + (east * pltpu.roll(q, lons - 1, 1) + west * pltpu.roll(q, 1, 1))
            new = new + (north * cells[r + 2, f] + south * cells[r, f])
            new = new + (below * q_below + above * q_above)
            store_row(f, new)

    def gather_first(r):
        load(r).wait()
        for f in range(field_count):
            first[r + 1, f, 0:levels, :] = raw[r, f]
        take_edges(0, first, r)

    def outer_rows(act):
        def body(i, carry):
            act(i * (rows - 1))
            return carry

        lax.fori_loop(0, 2, body, 0)

    def inner_rows(act):
        def body(r, carry):
            act(r)
            return carry

        lax.fori_loop(1, rows - 1, body, 0)

    outer_rows(gather_first)
    send_lat(0, first)
    inner_rows(gather_first)
    send_lev(0)
    wait_lev(0)
    wait_lat(0, first)

    def first_row(r):
        def put(f, value):
            second[r + 1, f] = value

        advance(0, r, first, put)
        take_edges(1, second, r)

    outer_rows(first_row)
    send_lat(1, second)
    inner_rows(first_row)
    send_lev(1)
    wait_lev(1)

    own = pl.ds(pl.multiple_of(me * quarter, quarter), quarter)

    def forward(r, d):
        peer = lax.rem(me + d, n)
        there = pl.ds(pl.multiple_of(peer * quarter, quarter), quarter)
        return pltpu.make_async_remote_copy(
            src_ref=state.at[r, :, :, there],
            dst_ref=held.at[r, me],
            send_sem=fsend.at[r, d - 1],
            recv_sem=frecv.at[r, d - 1],
            device_id={"lev": peer},
            device_id_type=MESH,
        )

    def backward(r, d):
        peer = lax.rem(me + d, n)
        return pltpu.make_async_remote_copy(
            src_ref=held.at[r, peer],
            dst_ref=out.at[r, :, :, own],
            send_sem=bsend.at[r, d - 1],
            recv_sem=brecv.at[r, d - 1],
            device_id={"lev": peer},
            device_id_type=MESH,
        )

    def second_row(r):
        def put(f, value):
            state[r, f] = value[:levels]

        advance(1, r, second, put)

    def send_forward(r):
        for d in range(1, n):
            forward(r, d).start()

    def second_and_send(r):
        second_row(r)
        send_forward(r)

    inner_rows(second_and_send)
    wait_lat(1, second)
    outer_rows(second_row)
    send_forward(0)
    column[...] = jnp.zeros(column.shape, jnp.float32)
    turn(w_up, up_t)
    turn(w_down, down_t)

    def one_row(i, carry):
        r = (i + 1) % (rows - 1) + (i // (rows - 1)) * (rows - 2)
        held[r, me] = state[r, :, :, own]
        for d in range(1, n):
            forward(r, d).wait_recv()

        @pl.when(i == 0)
        def _():
            send_forward(rows - 1)

        def substep(s, carry):
            x = column[...].reshape(n * field_count * slots, quarter)
            a = (x * inverse_rms(x, entries) * in_gain[...]).astype(jnp.bfloat16)
            h = dot(w_in[...], a)
            units = h.shape[0]
            g = (h * inverse_rms(h, units)).astype(jnp.bfloat16)
            v = dot(up_t[...], g)
            u = (v / (1.0 + jnp.exp(-v))).astype(jnp.bfloat16)
            h = h + dot(down_t[...], u)
            z = (h * inverse_rms(h, units) * out_gain[...]).astype(jnp.bfloat16)
            change = dot(w_out[...], z)
            x = x + jnp.where(classes[r] > s, change, 0.0)
            column[...] = x.reshape(n, field_count, slots, quarter)
            return carry

        for p in range(n):
            for f in range(field_count):
                column[p, f, 0:levels, :] = held[r, p, f]
        lax.fori_loop(0, SUBSTEPS, substep, 0)
        for p in range(n):
            for f in range(field_count):
                held[r, p, f] = column[p, f, 0:levels, :]
        out[r, :, :, own] = held[r, me]
        for d in range(1, n):
            backward(r, d).start()
        return carry

    lax.fori_loop(0, rows, one_row, 0)

    for r in (*inner, 0, rows - 1):
        for d in range(1, n):
            backward(r, d).wait_recv()
        store(r).start()
    for r in range(rows):
        for d in range(1, n):
            forward(r, d).wait_send()
            backward(r, d).wait_send()
    finish_sends(0, first)
    finish_sends(1, second)
    for r in range(rows):
        store(r).wait()


def on_device(
    fields,
    zonal_courant,
    merid_courant,
    vert_courant,
    column_class,
    in_gain,
    w_in,
    w_up,
    w_down,
    out_gain,
    w_out,
):
    field_count, levels_here, rows_here, lon_count = fields.shape
    n = lax.axis_size("lev")
    lat_index = lax.axis_index("lat")
    lev_index = lax.axis_index("lev")
    row_start = lat_index * rows_here
    lev_start = lev_index * levels_here
    inputs = w_in.shape[0]
    slots = -(-(levels_here + 1) // 16) * 16
    quarter = lon_count // n

    def by_source(array):
        tail = array.shape[1:]
        split = array.reshape((field_count, n, levels_here) + tail)
        split = jnp.moveaxis(split, 1, 0)
        split = jnp.pad(split, ((0, 0), (0, 0), (0, slots - levels_here)) + ((0, 0),) * len(tail))
        return split.reshape((n * field_count * slots,) + tail)

    gain_in = by_source(in_gain[:, None])
    w_in_t = by_source(w_in).T
    w_out_t = by_source(w_out.T)
    own_class = lax.dynamic_slice(
        column_class, (row_start, lev_index * quarter), (rows_here, quarter)
    ).reshape(rows_here, 1, quarter)
    coefs = face_coefficients(
        zonal_courant, merid_courant, vert_courant, lev_start, row_start, levels_here, rows_here
    )
    coefs = jnp.pad(coefs, ((0, 0), (0, slots - levels_here), (0, 0)))

    vmem = pl.BlockSpec(memory_space=pltpu.VMEM)
    hbm = pl.BlockSpec(memory_space=pl.ANY)
    pair = pltpu.SemaphoreType.DMA((STEPS, 2))
    grid = pltpu.SemaphoreType.DMA((rows_here, n - 1))
    single = pltpu.SemaphoreType.DMA((rows_here,))
    slab = (field_count, slots, lon_count)
    return pl.pallas_call(
        functools.partial(column_kernel, n, lax.axis_size("lat"), inputs),
        out_shape=jax.ShapeDtypeStruct(fields.shape, jnp.float32),
        in_specs=[hbm] + [vmem] * 8,
        out_specs=hbm,
        scratch_shapes=[
            pltpu.VMEM((n, field_count, slots, quarter), jnp.float32),
            pltpu.VMEM(w_up.shape[1:], w_up.dtype),
            pltpu.VMEM(w_down.shape[1:], w_down.dtype),
            pltpu.VMEM((rows_here, field_count, levels_here, lon_count), jnp.float32),
            pltpu.VMEM((rows_here + 2,) + slab, jnp.float32),
            pltpu.VMEM((rows_here + 2,) + slab, jnp.float32),
            pltpu.VMEM((rows_here, field_count, levels_here, lon_count), jnp.float32),
            pltpu.VMEM((rows_here, n, field_count, levels_here, quarter), jnp.float32),
            pltpu.VMEM((rows_here, field_count, levels_here, lon_count), jnp.float32),
            pltpu.VMEM((STEPS, 2, rows_here, field_count, lon_count), jnp.float32),
            pltpu.VMEM((STEPS, 2, rows_here, field_count, lon_count), jnp.float32),
            single, single, pair, pair, pair, pair, grid, grid, grid, grid,
        ],
        compiler_params=pltpu.CompilerParams(
            collective_id=0, has_side_effects=True, vmem_limit_bytes=48 * 2**20
        ),
    )(fields, coefs, own_class, gain_in, w_in_t, w_up[0], w_down[0], out_gain[:, None], w_out_t)


def solution(mesh):
    return jax.shard_map(
        on_device,
        mesh=mesh,
        in_specs=(P(None, "lev", "lat", None), P(), P(), P(), P(), P(), P(), P(), P(), P(), P()),
        out_specs=P(None, "lev", "lat", None),
        check_vma=False,
    )
```
